32 devices in a mesh: section: 2 (over core), wide: 4 (over z), narrow: 4 (over y, x).
Axes of the slice: x: 2, y: 2, z: 4, core: 2. Of those that a mesh axis runs over, the one named last changes fastest.
Arguments:
- block_input: bfloat16 [2, 960, 4096], P(None, 'narrow', 'wide'), may hold values from -6 to 6
- output_cotangent: bfloat16 [2, 960, 4096], P(None, 'narrow', 'wide'), may hold values from -6 to 6
- segment_ids: int32 [2, 4096], P(None, 'wide'), may hold values from 0 to 4, as said below
- first_gain: bfloat16 [2, 960], P('section', 'narrow'), may hold values from 0.25 to 1.75
- w_query: bfloat16 [2, 960, 960], P('section', 'wide', 'narrow'), may hold values from -0.25 to 0.25
- w_key: bfloat16 [2, 960, 320], P('section', 'wide', 'narrow'), may hold values from -0.1875 to 0.1875
- w_value: bfloat16 [2, 960, 320], P('section', 'wide', 'narrow'), may hold values from -0.1875 to 0.1875
- w_out: bfloat16 [2, 960, 960], P('section', 'narrow', 'wide'), may hold values from -1.5 to 1.5
- second_gain: bfloat16 [2, 960], P('section', 'narrow'), may hold values from 0.25 to 1.75
- w_gate: bfloat16 [2, 960, 2560], P('section', 'wide', 'narrow'), may hold values from -0.1875 to 0.1875
- w_up: bfloat16 [2, 960, 2560], P('section', 'wide', 'narrow'), may hold values from -0.1875 to 0.1875
- w_down: bfloat16 [2, 2560, 960], P('section', 'narrow', 'wide'), may hold values from -0.125 to 0.125
Outputs:
- section_outputs: bfloat16 [2, 2, 960, 4096], P('section', None, 'narrow', 'wide')
- input_grads: bfloat16 [2, 2, 960, 4096], P('section', None, 'narrow', 'wide')
- grad_first_gain: float32 [2, 960], P('section', 'narrow')
- grad_query: float32 [2, 960, 960], P('section', 'wide', 'narrow')
- grad_key: float32 [2, 960, 320], P('section', 'wide', 'narrow')
- grad_value: float32 [2, 960, 320], P('section', 'wide', 'narrow')
- grad_out: float32 [2, 960, 960], P('section', 'narrow', 'wide')
- grad_second_gain: float32 [2, 960], P('section', 'narrow')
- grad_gate: float32 [2, 960, 2560], P('section', 'wide', 'narrow')
- grad_up: float32 [2, 960, 2560], P('section', 'wide', 'narrow')
- grad_down: float32 [2, 2560, 960], P('section', 'narrow', 'wide')
The draws below stay inside these ranges and needn't reach their ends.
Inputs may be any that keep to these rules, and one draw needn't show every extreme that they name: `segment_ids`: within each sequence of 1024 tokens the ids start at 0 and never fall; in each sequence one document begins among its first 256 tokens and ends among its last 256 tokens.
All inputs are finite; a program needn't handle non-finite values.
Results may differ from the reference program's by a relative error of at most 0.04.
Values may be sent and summed in bfloat16 or wider, within the bound.
A program may use at most 256 MiB of HBM per device.

```python
import jax
import jax.numpy as jnp
from jax import lax

D = 960
HEADS = 15
KV_HEADS = 5
HEAD = 64
FF = 2560
SEQ = 1024
MB = 2
TOKENS = 4096
SECTIONS = 2
N_SECTION = 2


def draw_segment_ids(key, part):
    key = jax.random.fold_in(key, 7)
    count_seq = MB * (TOKENS // SEQ)
    quarter = SEQ // 4
    key_one, key_two, key_three, key_four = jax.random.split(key, 4)
    begin = jax.random.randint(key_one, (count_seq, 1), 2, quarter)
    first_cut = jax.random.randint(key_two, (count_seq, 1), 1, begin)
    finish = jax.random.randint(key_three, (count_seq, 1), 3 * quarter + 1, SEQ)
    last_cut = jax.random.randint(key_four, (count_seq, 1), finish, SEQ)
    places = jnp.arange(SEQ, dtype=jnp.int32)[None, :]
    labels = (places >= first_cut).astype(jnp.int32) + (places >= begin).astype(jnp.int32)
    labels = labels + (places >= finish).astype(jnp.int32) + (places >= last_cut).astype(jnp.int32)
    return labels.reshape(MB, TOKENS)


def block_levels(own_key, extent, cuts, smallest, high):
    level = 1.0
    for dim, parts in cuts:
        heights = jax.random.uniform(jax.random.fold_in(jax.random.fold_in(own_key, 6), dim), (parts,), jnp.float32, smallest / len(cuts), high / len(cuts))
        level = level * jnp.repeat(jnp.exp(heights), extent[dim] // parts).reshape((-1,) + (1,) * (len(extent) - 1 - dim))
    return level


def noise(stream_key, shape, width, reach, cuts=(), kind=jnp.bfloat16):
    gain = block_levels(stream_key, shape, cuts, -0.22, 0.18) if cuts else 1.0
    drawn = jax.random.normal(stream_key, shape, jnp.float32) * width * gain
    return jnp.minimum(jnp.maximum(drawn, -reach), reach).astype(kind)


def setup_inputs(seed: int = 0) -> dict:
    keys = jax.random.split(jax.random.key(seed), 13)
    return {
        "block_input": noise(keys[0], (MB, D, TOKENS), 1.0, 6.0, ((1, 4), (2, 4))),
        "output_cotangent": noise(keys[1], (MB, D, TOKENS), 1.0, 6.0, ((1, 4), (2, 4))),
        "segment_ids": draw_segment_ids(jax.random.fold_in(keys[12], 71), 0),
        "first_gain": jnp.clip(1.0 + 0.15 * jax.random.normal(keys[3], (SECTIONS, D), jnp.float32), 0.25, 1.75).astype(jnp.bfloat16),
        "w_query": noise(keys[4], (SECTIONS, D, D), (D // 2) ** -0.5, 0.25, ((0, 2), (1, 4), (2, 4))),
        "w_key": noise(keys[5], (SECTIONS, D, KV_HEADS * HEAD), D ** -0.5, 0.1875, ((0, 2), (1, 4), (2, 4))),
        "w_value": noise(keys[6], (SECTIONS, D, KV_HEADS * HEAD), D ** -0.5, 0.1875, ((0, 2), (1, 4), (2, 4))),
        "w_out": noise(keys[7], (SECTIONS, D, D), (D // 64) ** -0.5, 1.5, ((0, 2), (1, 4), (2, 4))),
        "second_gain": jnp.clip(1.0 + 0.15 * jax.random.normal(keys[8], (SECTIONS, D), jnp.float32), 0.25, 1.75).astype(jnp.bfloat16),
        "w_gate": noise(keys[9], (SECTIONS, D, FF), D ** -0.5, 0.1875, ((0, 2), (1, 4), (2, 4))),
        "w_up": noise(keys[10], (SECTIONS, D, FF), D ** -0.5, 0.1875, ((0, 2), (1, 4), (2, 4))),
        "w_down": noise(keys[11], (SECTIONS, FF, D), FF ** -0.5, 0.125, ((0, 2), (1, 4), (2, 4))),
    }


EPSILON = 1e-05
ROPE_BASE = 100000.0
NEG_FILL = -1e+30
id_levels = 5
HIGHEST = lax.Precision.HIGHEST

@jax.custom_vjp
def low(v):
    return lax.optimization_barrier(v.astype(jnp.bfloat16)).astype(jnp.float32)

@jax.custom_vjp
def low_back(v):
    return v

def low_keep(v):
    return (low(v), None)

def low_pass(kept, grad):
    return (grad,)

def back_keep(v):
    return (v, None)

def back_low(kept, grad):
    return (low(grad),)
low.defvjp(low_keep, low_pass)
low_back.defvjp(back_keep, back_low)

def matmul(left, right):
    return jnp.dot(left, right, precision=HIGHEST)

def tables(segment_row):
    length = segment_row.shape[0]
    levels = jnp.arange(id_levels, dtype=jnp.int32)
    onehot = (segment_row[:, None] == levels[None, :]).astype(jnp.float32)
    counts = lax.optimization_barrier(jnp.sum(onehot, axis=0))
    starts = jnp.cumsum(counts) - counts
    doc_start = lax.optimization_barrier(jnp.sum(onehot * starts[None, :], axis=1))
    doc_place = jnp.arange(length, dtype=jnp.float32) - doc_start
    half_head = HEAD // 2
    inverse = ROPE_BASE ** (-jnp.arange(half_head, dtype=jnp.float32) / half_head)
    angles = doc_place[:, None] * inverse[None, :]
    return (jnp.cos(angles), jnp.sin(angles))

def rotate(values, cosine, sine_table):
    row_count = values.shape[0]
    head_count = values.shape[1] // HEAD
    half_head = HEAD // 2
    shaped = values.reshape(row_count, head_count, HEAD)
    first_half = shaped[:, :, :half_head]
    second = shaped[:, :, half_head:]
    cos_part = cosine[:, None, :]
    sin_part = sine_table[:, None, :]
    turned = jnp.concatenate([first_half * cos_part - second * sin_part, second * cos_part + first_half * sin_part], axis=2)
    return turned.reshape(row_count, head_count * HEAD)

def layer(inputs, params, cosine, sine_table, allowed):
    norm_one, w_query, w_key, w_value, w_out, norm_two, w_gate, w_up, w_down = params
    length = inputs.shape[0]
    groups = HEADS // KV_HEADS
    score_scale = HEAD ** (-0.5)
    rstd_one = lax.rsqrt(lax.optimization_barrier(jnp.mean(inputs * inputs, axis=-1, keepdims=True)) + EPSILON)
    normed = low(inputs * rstd_one * norm_one)
    query_pre = low_back(low(matmul(normed, w_query)))
    key_pre = low_back(low(matmul(normed, w_key)))
    value_all = low_back(low(matmul(normed, w_value)))
    queries = low(rotate(query_pre, cosine, sine_table)).reshape(length, KV_HEADS, groups, HEAD)
    keys_rot = low(rotate(key_pre, cosine, sine_table)).reshape(length, KV_HEADS, HEAD)
    values = value_all.reshape(length, KV_HEADS, HEAD)
    scores = low_back(jnp.einsum('qgjd,kgd->gjqk', queries, keys_rot, precision=HIGHEST) * score_scale)
    scores = jnp.where(allowed[None, None], scores, NEG_FILL)
    row_top = lax.optimization_barrier(jnp.max(scores, axis=-1, keepdims=True))
    exp_scores = jnp.exp(scores - row_top)
    probs_low = low(exp_scores / lax.optimization_barrier(jnp.sum(exp_scores, axis=-1, keepdims=True)))
    mixed = jnp.einsum('gjqk,kgd->qgjd', probs_low, values, precision=HIGHEST).reshape(length, HEADS * HEAD)
    mixed = low_back(low(mixed))
    branch = low_back(matmul(mixed, w_out))
    middle = inputs + branch
    rstd_two = lax.rsqrt(lax.optimization_barrier(jnp.mean(middle * middle, axis=-1, keepdims=True)) + EPSILON)
    normed_two = low(middle * rstd_two * norm_two)
    gate_values = low_back(matmul(normed_two, w_gate))
    up_values = low_back(matmul(normed_two, w_up))
    hidden = low(jax.nn.silu(gate_values) * up_values)
    return middle + matmul(hidden, w_down)

def stack_forward(inputs, probes, params_all, cosine, sine_table, allowed):
    current = inputs
    results = []
    for section_number in range(N_SECTION):
        if section_number > 0:
            current = low_back(current)
        current = current + probes[section_number]
        params = tuple((entry[section_number] for entry in params_all))
        current = low(layer(current, params, cosine, sine_table, allowed))
        results.append(current)
    return jnp.stack(results)

def reference(block_input, output_cotangent, segment_ids, first_gain, w_query, w_key, w_value, w_out, second_gain, w_gate, w_up, w_down):
    count_seq = TOKENS // SEQ
    units = MB * count_seq
    inputs = jnp.transpose(block_input.astype(jnp.float32), (0, 2, 1)).reshape(units, SEQ, D)
    cotangent = jnp.transpose(output_cotangent.astype(jnp.float32), (0, 2, 1)).reshape(units, SEQ, D)
    segments = segment_ids.reshape(units, SEQ)
    params_all = tuple((entry.astype(jnp.float32) for entry in (first_gain, w_query, w_key, w_value, w_out, second_gain, w_gate, w_up, w_down)))
    positions = jnp.arange(SEQ, dtype=jnp.int32)

    def per_sequence(totals, item_set):
        seq_in, seq_cot, seq_ids = item_set
        cosine, sine_table = tables(seq_ids)
        allowed = (seq_ids[:, None] == seq_ids[None, :]) & (positions[None, :] <= positions[:, None])
        probes = jnp.zeros((N_SECTION, SEQ, D), jnp.float32)

        def wrapped(first_in, probe_set, param_set):
            return stack_forward(first_in, probe_set, param_set, cosine, sine_table, allowed)
        results, pullback = jax.vjp(wrapped, seq_in, probes, params_all)
        seed_grad = jnp.zeros_like(results).at[N_SECTION - 1].set(seq_cot)
        unused_grad, probe_grads, param_grads = pullback(seed_grad)
        totals = jax.tree.map(jnp.add, totals, param_grads)
        return (totals, (results, probe_grads))
    start_totals = jax.tree.map(jnp.zeros_like, params_all)
    totals, (results, probe_grads) = lax.scan(per_sequence, start_totals, (inputs, cotangent, segments))

    def arrange(stacked):
        shaped = stacked.reshape(MB, count_seq, N_SECTION, SEQ, D)
        ordered = jnp.transpose(shaped, (2, 0, 4, 1, 3))
        return ordered.reshape(N_SECTION, MB, D, TOKENS).astype(jnp.bfloat16)
    grad_gain_one, grad_query_w, grad_key_w, grad_value_w, grad_out_w, grad_gain_two, grad_gate_w, grad_up_w, grad_down_w = totals
    return (arrange(results), arrange(probe_grads), grad_gain_one, grad_query_w, grad_key_w, grad_value_w, grad_out_w, grad_gain_two, grad_gate_w, grad_up_w, grad_down_w)
```

```python
import functools

import jax
import jax.numpy as jnp
from jax import lax
from jax.experimental import pallas as pl
from jax.experimental.pallas import tpu as pltpu
from jax.sharding import PartitionSpec as P

HEAD = 64
EPSILON = 1e-05
ROPE_BASE = 100000.0
NEG_FILL = -1e30
LOW = jnp.bfloat16
FULL = jnp.float32
SCALE = HEAD ** (-0.5)


def dot(left, right, left_dim, right_dim):
    return lax.dot_general(
        left, right, (((left_dim,), (right_dim,)), ((), ())), preferred_element_type=FULL
    )


def attend_kernel(blocks, groups, q_ref, k_ref, v_ref, mask_ref, mixed_ref, log_ref):
    length = q_ref.shape[1]
    for member in range(groups):
        rows = pl.ds(member * HEAD, HEAD)
        query = q_ref[rows, :]
        scores = []
        for j in range(blocks):
            allowed = mask_ref[pl.ds(j * length, length), :] > 0
            scores.append(jnp.where(allowed, dot(k_ref[j, 0], query, 0, 0) * SCALE, NEG_FILL))
        top = scores[0].max(axis=0, keepdims=True)
        for j in range(1, blocks):
            top = jnp.maximum(top, scores[j].max(axis=0, keepdims=True))
        scores = [jnp.exp(s - top) for s in scores]
        total = sum(s.sum(axis=0, keepdims=True) for s in scores)
        inverse = 1.0 / total
        mixed = sum(
            dot(v_ref[j, 0], (scores[j] * inverse).astype(LOW), 1, 0) for j in range(blocks)
        )
        mixed_ref[rows, :] = mixed.astype(LOW)
        log_ref[0, pl.ds(member, 1), :] = top + jnp.log(total)


def attend_back_kernel(
    blocks, groups, q_ref, k_ref, v_ref, mask_ref, log_ref, grad_ref, dq_ref, dk_ref, dv_ref
):
    length = q_ref.shape[1]
    dk = [0.0] * blocks
    dv = [0.0] * blocks
    for member in range(groups):
        rows = pl.ds(member * HEAD, HEAD)
        query = q_ref[rows, :]
        grad = grad_ref[rows, :]
        logs = log_ref[0, pl.ds(member, 1), :]
        probs = []
        grads = []
        delta = 0.0
        for j in range(blocks):
            allowed = mask_ref[pl.ds(j * length, length), :] > 0
            score = jnp.where(allowed, dot(k_ref[j, 0], query, 0, 0) * SCALE, NEG_FILL)
            prob = jnp.exp(score - logs)
            grad_prob = dot(v_ref[j, 0], grad, 0, 0)
            delta = delta + (prob * grad_prob).sum(axis=0, keepdims=True)
            probs.append(prob)
            grads.append(grad_prob)
        dq = 0.0
        for j in range(blocks):
            low_score = (probs[j] * (grads[j] - delta)).astype(LOW)
            dq = dq + dot(k_ref[j, 0], low_score, 1, 0)
            dk[j] = dk[j] + dot(query, low_score, 1, 1)
            dv[j] = dv[j] + dot(grad, probs[j].astype(LOW), 1, 1)
        dq_ref[rows, :] = dq * SCALE
    for j in range(blocks):
        dk_ref[j, 0] = (dk[j] * SCALE).astype(LOW)
        dv_ref[j, 0] = dv[j].astype(LOW)


def attention_specs(blocks, kv_heads, groups, length):
    head_rows = pl.BlockSpec((groups * HEAD, length), lambda g: (g, 0))
    kv = pl.BlockSpec((blocks, 1, HEAD, length), lambda g: (0, g, 0, 0))
    mask = pl.BlockSpec((blocks * length, length), lambda g: (0, 0))
    logs = pl.BlockSpec((1, groups, length), lambda g: (g, 0, 0))
    return head_rows, kv, mask, logs


def attend(queries, keys, values, mask):
    blocks, kv_heads, _, length = keys.shape
    groups = queries.shape[0] // (kv_heads * HEAD)
    head_rows, kv, mask_spec, logs = attention_specs(blocks, kv_heads, groups, length)
    return pl.pallas_call(
        functools.partial(attend_kernel, blocks, groups),
        grid=(kv_heads,),
        in_specs=[head_rows, kv, kv, mask_spec],
        out_specs=[head_rows, logs],
        out_shape=[
            jax.ShapeDtypeStruct(queries.shape, LOW),
            jax.ShapeDtypeStruct((kv_heads, groups, length), FULL),
        ],
        compiler_params=pltpu.CompilerParams(vmem_limit_bytes=32 << 20),
        cost_estimate=pl.CostEstimate(
            flops=16 * queries.size * blocks * length, bytes_accessed=8 << 20, transcendentals=0
        ),
    )(queries, keys, values, mask)


def attend_back(queries, keys, values, mask, logs, grad):
    blocks, kv_heads, _, length = keys.shape
    groups = queries.shape[0] // (kv_heads * HEAD)
    head_rows, kv, mask_spec, log_spec = attention_specs(blocks, kv_heads, groups, length)
    return pl.pallas_call(
        functools.partial(attend_back_kernel, blocks, groups),
        grid=(kv_heads,),
        in_specs=[head_rows, kv, kv, mask_spec, log_spec, head_rows],
        out_specs=[head_rows, kv, kv],
        out_shape=[
            jax.ShapeDtypeStruct(queries.shape, FULL),
            jax.ShapeDtypeStruct(keys.shape, LOW),
            jax.ShapeDtypeStruct(keys.shape, LOW),
        ],
        compiler_params=pltpu.CompilerParams(vmem_limit_bytes=32 << 20),
        cost_estimate=pl.CostEstimate(
            flops=40 * queries.size * blocks * length, bytes_accessed=8 << 20, transcendentals=0
        ),
    )(queries, keys, values, mask, logs, grad)


def rotate(values, cosine, sine):
    length = values.shape[1]
    shaped = values.reshape(-1, 2, HEAD // 2, length)
    a, b = shaped[:, 0], shaped[:, 1]
    return jnp.stack([a * cosine - b * sine, b * cosine + a * sine], axis=1).reshape(values.shape)


def inverse_rms(values):
    return lax.rsqrt(jnp.mean(values * values, axis=0, keepdims=True) + EPSILON)


def norm_back(grad_normed, source, rstd, gain):
    scaled = grad_normed * gain
    row = jnp.mean(scaled * source, axis=0, keepdims=True)
    return rstd * scaled - source * rstd**3 * row


def reduce_scatter(blocks, axis):
    size = lax.axis_size(axis)
    me = lax.axis_index(axis)
    total = lax.dynamic_index_in_dim(blocks, me, 0, keepdims=False).astype(FULL)
    power = size & (size - 1) == 0
    for step in range(1, size):
        if power:
            pairs = [(i, i ^ step) for i in range(size)]
            target = me ^ step
        else:
            pairs = [(i, (i + step) % size) for i in range(size)]
            target = (me + step) % size
        sent = lax.dynamic_index_in_dim(blocks, target, 0, keepdims=False)
        total = total + lax.ppermute(sent, axis, pairs).astype(FULL)
    return total


def local(
    block_input,
    output_cotangent,
    segment_ids,
    first_gain,
    w_query,
    w_key,
    w_value,
    w_out,
    second_gain,
    w_gate,
    w_up,
    w_down,
):
    everywhere = ("section", "narrow", "wide")
    sections = lax.axis_size("section")
    narrow = lax.axis_size("narrow")
    wide = lax.axis_size("wide")
    core = lax.axis_index("section")
    place = lax.axis_index("narrow")
    features = block_input.shape[1]
    width = features * narrow
    sequence = block_input.shape[2]
    length = sequence // narrow
    q_cols, k_cols, hidden_cols = w_query.shape[2], w_key.shape[2], w_gate.shape[2]
    kv_heads = k_cols * narrow // HEAD
    qkv_cols = q_cols + 2 * k_cols
    half = qkv_cols + q_cols + hidden_cols
    gate_at = qkv_cols + q_cols

    packed = jnp.stack(
        [
            jnp.concatenate([w_query[0], w_key[0], w_value[0], w_out[0].T, w_gate[0]], axis=1),
            jnp.concatenate([w_up[0], w_down[0].T], axis=1),
        ]
    )
    halves = lax.all_to_all(packed, "section", 0, 0, tiled=True)
    weights = [
        lax.all_gather(halves[layer], everywhere, axis=0, tiled=True).reshape(
            2, narrow, width, half
        )
        for layer in range(sections)
    ]

    gains = lax.all_gather(
        jnp.stack([first_gain[0], second_gain[0]]), ("section", "narrow"), axis=0
    ).reshape(sections, narrow, 2, features)
    gains = jnp.transpose(gains, (0, 2, 1, 3)).reshape(sections, 2, width, 1).astype(FULL)

    ends = jnp.stack(
        [
            lax.dynamic_index_in_dim(block_input, core, 0, keepdims=False),
            lax.dynamic_index_in_dim(output_cotangent, core, 0, keepdims=False),
        ]
    ).reshape(2, features, narrow, length)
    ends = lax.all_to_all(jnp.transpose(ends, (2, 0, 1, 3)), "narrow", 0, 0, tiled=True)
    start = ends[:, 0].reshape(width, length)
    cotangent = ends[:, 1].reshape(width, length)

    ids = lax.dynamic_index_in_dim(segment_ids, core, 0, keepdims=False)
    offset = place * length
    own_ids = lax.dynamic_slice_in_dim(ids, offset, length, 0)
    positions = jnp.arange(sequence, dtype=jnp.int32)
    own_positions = offset + jnp.arange(length, dtype=jnp.int32)
    mask = (
        (ids[:, None] == own_ids[None, :]) & (positions[:, None] <= own_positions[None, :])
    ).astype(FULL)
    doc_start = jnp.sum((ids[:, None] < own_ids[None, :]).astype(FULL), axis=0)
    half_head = HEAD // 2
    inverse = ROPE_BASE ** (-jnp.arange(half_head, dtype=FULL) / half_head)
    angles = inverse[:, None] * (own_positions.astype(FULL) - doc_start)[None, :]
    cosine, sine = jnp.cos(angles), jnp.sin(angles)

    def q_part(values, n):
        return values[n * q_cols : (n + 1) * q_cols]

    def k_part(values, n):
        return values[n * k_cols : (n + 1) * k_cols]

    kept = []
    results = []
    source = start.astype(FULL)
    for layer in range(sections):
        first, second = weights[layer][0], weights[layer][1]
        gain_one, gain_two = gains[layer, 0], gains[layer, 1]
        rstd_one = inverse_rms(source)
        normed = (source * rstd_one * gain_one).astype(LOW)
        qkv = [dot(first[n, :, :qkv_cols], normed, 0, 0).astype(LOW) for n in range(narrow)]
        query = jnp.concatenate([b[:q_cols] for b in qkv])
        key = jnp.concatenate([b[q_cols : q_cols + k_cols] for b in qkv])
        value = jnp.concatenate([b[q_cols + k_cols :] for b in qkv])
        queries = rotate(query.astype(FULL), cosine, sine).astype(LOW)
        keys = rotate(key.astype(FULL), cosine, sine).astype(LOW)
        both = lax.all_gather(jnp.stack([keys, value]), "narrow", axis=0)
        both = both.reshape(narrow, 2, kv_heads, HEAD, length)
        key_all, value_all = both[:, 0], both[:, 1]
        mixed, logs = attend(queries, key_all, value_all, mask)
        middle = source
        for n in range(narrow):
            middle = middle + dot(first[n, :, qkv_cols:gate_at], q_part(mixed, n), 1, 0)
        rstd_two = inverse_rms(middle)
        normed_two = (middle * rstd_two * gain_two).astype(LOW)
        gates, ups, hiddens = [], [], []
        result = middle
        for n in range(narrow):
            gate = dot(first[n, :, gate_at:], normed_two, 0, 0)
            up = dot(second[n, :, :hidden_cols], normed_two, 0, 0)
            hidden = (jax.nn.silu(gate) * up).astype(LOW)
            result = result + dot(second[n, :, hidden_cols:], hidden, 1, 0)
            gates.append(gate)
            ups.append(up)
            hiddens.append(hidden)
        result = result.astype(LOW)
        kept.append(
            (source, rstd_one, normed, queries, key_all, value_all, mixed, logs, middle)
            + (rstd_two, normed_two, gates, ups, hiddens)
        )
        results.append(result)
        source = result.astype(FULL)

    input_grads = [None] * sections
    gain_grads = [None] * sections
    weight_shards = [None] * sections
    grad = cotangent
    for layer in reversed(range(sections)):
        first, second = weights[layer][0], weights[layer][1]
        gain_one, gain_two = gains[layer, 0], gains[layer, 1]
        (source, rstd_one, normed, queries, key_all, value_all, mixed, logs, middle) = kept[layer][
            :9
        ]
        rstd_two, normed_two, gates, ups, hiddens = kept[layer][9:]
        grad_normed = 0.0
        gate_terms, second_terms = [], []
        for n in range(narrow):
            grad_hidden = dot(second[n, :, hidden_cols:], grad, 0, 0)
            sig = jax.nn.sigmoid(gates[n])
            grad_gate = (grad_hidden * ups[n] * sig * (1.0 + gates[n] * (1.0 - sig))).astype(LOW)
            grad_up = (grad_hidden * gates[n] * sig).astype(LOW)
            grad_normed = grad_normed + dot(first[n, :, gate_at:], grad_gate, 1, 0)
            grad_normed = grad_normed + dot(second[n, :, :hidden_cols], grad_up, 1, 0)
            gate_terms.append(dot(normed_two, grad_gate, 1, 1).astype(LOW))
            second_terms.append(
                jnp.concatenate(
                    [
                        dot(normed_two, grad_up, 1, 1).astype(LOW),
                        dot(grad, hiddens[n], 1, 1).astype(LOW),
                    ],
                    axis=1,
                )
            )
        grad_gain_two = jnp.sum(grad_normed * middle * rstd_two, axis=1)
        grad_middle = grad.astype(FULL) + norm_back(grad_normed, middle, rstd_two, gain_two)
        branch = grad_middle.astype(LOW)
        grad_mixed = jnp.concatenate(
            [dot(first[n, :, qkv_cols:gate_at], branch, 0, 0).astype(LOW) for n in range(narrow)]
        )
        grad_query, grad_key, grad_value = attend_back(
            queries, key_all, value_all, mask, logs, grad_mixed
        )
        sums = lax.all_to_all(
            jnp.stack([grad_key, grad_value], axis=1), "narrow", 0, 0, tiled=True
        )
        sums = jnp.sum(sums.astype(FULL), axis=0).reshape(2, kv_heads * HEAD, length)
        dq = rotate(grad_query, cosine, -sine).astype(LOW)
        dk = rotate(sums[0], cosine, -sine).astype(LOW)
        dv = sums[1].astype(LOW)
        grad_normed = 0.0
        terms = []
        for n in range(narrow):
            block = jnp.concatenate([q_part(dq, n), k_part(dk, n), k_part(dv, n)])
            grad_normed = grad_normed + dot(first[n, :, :qkv_cols], block, 1, 0)
            first_term = jnp.concatenate(
                [
                    dot(normed, block, 1, 1).astype(LOW),
                    dot(branch, q_part(mixed, n), 1, 1).astype(LOW),
                    gate_terms[n],
                ],
                axis=1,
            )
            terms.append(first_term)
        grad_gain_one = jnp.sum(grad_normed * source * rstd_one, axis=1)
        grad = (grad_middle + norm_back(grad_normed, source, rstd_one, gain_one)).astype(LOW)
        input_grads[layer] = grad
        gain_grads[layer] = jnp.stack([grad_gain_one, grad_gain_two])
        stacked = jnp.stack([jnp.stack(terms), jnp.stack(second_terms)])
        shard = reduce_scatter(stacked, "section").astype(LOW)
        shard = reduce_scatter(shard, "narrow").astype(LOW)
        shard = reduce_scatter(shard.reshape(wide, width // wide, half), "wide")
        weight_shards[layer] = shard.astype(LOW)

    owned = lax.all_to_all(jnp.stack(weight_shards), "section", 0, 0, tiled=True).astype(FULL)
    first, second = owned[0], owned[1]

    gain_total = lax.psum(jnp.stack(gain_grads), everywhere)
    gain_total = lax.dynamic_index_in_dim(gain_total, core, 0, keepdims=False)
    gain_total = lax.dynamic_slice_in_dim(gain_total, place * features, features, 1)

    ends = jnp.stack([jnp.stack(results), jnp.stack(input_grads)], axis=1)
    ends = ends.reshape(sections, 2, narrow, features, length)
    ends = jnp.transpose(ends, (0, 2, 1, 3, 4)).reshape(-1, 2, features, length)
    ends = lax.all_to_all(ends, ("section", "narrow"), 0, 0, tiled=True)
    ends = ends.reshape(sections, narrow, 2, features, length)
    ends = jnp.transpose(ends, (2, 0, 3, 1, 4)).reshape(2, sections, features, sequence)

    k_at, v_at = q_cols, q_cols + k_cols
    return (
        ends[0][None],
        ends[1][None],
        gain_total[0][None],
        first[:, :q_cols][None],
        first[:, k_at:v_at][None],
        first[:, v_at:qkv_cols][None],
        first[:, qkv_cols:gate_at].T[None],
        gain_total[1][None],
        first[:, gate_at:][None],
        second[:, :hidden_cols][None],
        second[:, hidden_cols:].T[None],
    )


def solution(mesh):
    by_rows = P("section", "wide", "narrow")
    by_columns = P("section", "narrow", "wide")
    gain = P("section", "narrow")
    ends = P(None, "narrow", "wide")
    in_specs = (
        (ends, ends, P(None, "wide"), gain)
        + (by_rows, by_rows, by_rows, by_columns, gain)
        + (by_rows, by_rows, by_columns)
    )
    carried = P("section", None, "narrow", "wide")
    out_specs = (
        (carried, carried, gain)
        + (by_rows, by_rows, by_rows, by_columns, gain)
        + (by_rows, by_rows, by_columns)
    )
    return jax.shard_map(local, mesh=mesh, in_specs=in_specs, out_specs=out_specs, check_vma=False)
```
